32 devices in a mesh: groups: 2 (over y), blk: 4 (over z), ulysses: 2 (over x), cfg: 2 (over core).
Axes of the slice: x: 2, y: 2, z: 4, core: 2. Of those that a mesh axis runs over, the one named last changes fastest.
Arguments:
- queries: bfloat16 [2, 256, 3072], P('cfg', ('groups', 'blk', 'ulysses')), parts along dimension 1, may hold values from -330 to 330
- key_now: bfloat16 [2, 256, 3072], P('cfg', ('groups', 'blk', 'ulysses')), parts along dimension 1, may hold values from -6 to 6
- value_now: bfloat16 [2, 256, 3072], P('cfg', ('groups', 'blk', 'ulysses')), parts along dimension 1, may hold values from -6 to 6
- key_stale: bfloat16 [2, 256, 3072], P('cfg', 'groups', 'ulysses'), parts along dimension 1, may hold values from -6 to 6
- value_stale: bfloat16 [2, 256, 3072], P('cfg', 'groups', 'ulysses'), parts along dimension 1, may hold values from -6 to 6
- positions: int32 [256], P(('groups', 'blk', 'ulysses')), parts along dimension 0, may hold values from 0 to 127, each once
- exponents: int32 [2, 2, 8, 24], P(None, 'cfg', 'groups', 'ulysses'), parts along dimension 2, may hold values from -9 to -4
- step_index: int32 [100], P('groups'), parts along dimension 0, may hold values from 0 to 49, each once
- step_gates: bfloat16 [50, 3072], P(None, 'ulysses'), may hold values from 0.5 to 2
Outputs:
- attended: bfloat16 [2, 256, 3072], P('cfg', ('groups', 'blk', 'ulysses')), parts along dimension 1
The draws below stay inside these ranges and needn't reach their ends.
There are 2 independent parts, one for each index of `groups`. The reference program is written for one: setup_inputs(seed, part) draws one part's arguments, and reference() takes and returns one part's arrays. A program takes and returns all parts, laid end to end along the dimension named above; an argument that names none is the same for every part. Nothing has to cross between parts.
Inputs may be any that keep to these rules, and one draw needn't show every extreme that they name: positions hold every number below 128 once. step_index holds every number below 50 once.
All inputs are finite; a program needn't handle non-finite values.
Results may differ from the reference program's by a relative error of at most 0.012.
The reference program's roundings to bfloat16 on the way (of `weights`) count: a program that leaves them out, or rounds other values in their place, can miss the bound.
Values may be sent and summed in bfloat16 or wider, within the bound.
A program may use at most 64 MiB of HBM per device.

```python
import math
import jax
import jax.numpy as jnp
from jax import lax

HEADS = 24
HD = 128
BLOCK = 32
STEPS = 50
GRID_H = 16
GRID_W = 16
TOKENS = 128
NBLOCKS = 4


def draw_queries(key, part):
    key = jax.random.fold_in(key, 11)
    shape = (2, TOKENS, HEADS * HD)
    values = 2.5 * jax.random.truncated_normal(key, -4.0, 4.0, shape, jnp.float32)
    return values.astype(jnp.bfloat16)


def set_ends(drawn, stream_key, low, largest):
    shape = drawn.shape
    place = [jax.random.randint(jax.random.fold_in(stream_key, axis), (), 0, shape[axis]) for axis in range(len(shape))]
    drawn = drawn.at[tuple(place)].set(low)
    longest = shape.index(max(shape))
    place[longest] = (place[longest] + 1) % shape[longest]
    return drawn.at[tuple(place)].set(largest)


def block_levels(key, dims, cuts, smallest, high):
    factor_of, own = 1.0, jax.random.fold_in(key, 6)
    for axis_at, blocks in cuts:
        steps = jnp.exp(jax.random.uniform(jax.random.fold_in(own, axis_at), (blocks,), jnp.float32, smallest / len(cuts), high / len(cuts)))
        factor_of = factor_of * jnp.repeat(steps, dims[axis_at] // blocks).reshape([-1 if axis == axis_at else 1 for axis in range(len(dims))])
    return factor_of


def gaussian(stream_key, dims, width, limit, shards=(), held_as=jnp.bfloat16):
    values = jax.random.normal(stream_key, dims, jnp.float32) * width
    if len(shards) > 0:
        values = block_levels(stream_key, dims, shards, -0.22, 0.18) * values
    return jnp.clip(values, min=-limit, max=limit).astype(held_as)


def setup_inputs(seed: int = 0, part: int = 0) -> dict:
    key_of = jax.random.split(jax.random.key(seed), 10)
    own_keys = jax.random.split(jax.random.fold_in(key_of[9], part), 10)
    return {
        "queries": draw_queries(jax.random.fold_in(jax.random.fold_in(key_of[9], part), 71), part),
        "key_now": gaussian(own_keys[1], (2, TOKENS, HEADS * HD), 1.0, 6.0, ((0, 2), (1, 8))),
        "value_now": gaussian(own_keys[2], (2, TOKENS, HEADS * HD), 1.0, 6.0, ((0, 2), (1, 8))),
        "key_stale": gaussian(own_keys[3], (2, TOKENS, HEADS * HD), 1.0, 6.0, ((0, 2), (2, 2))),
        "value_stale": gaussian(own_keys[4], (2, TOKENS, HEADS * HD), 1.0, 6.0, ((0, 2), (2, 2))),
        "positions": jax.random.permutation(own_keys[5], TOKENS).astype(jnp.int32),
        "exponents": set_ends(jax.random.randint(own_keys[6], (2, 2, NBLOCKS, HEADS), -9, -3), jax.random.fold_in(own_keys[6], 1), -9, (-3) - 1).astype(jnp.int32),
        "step_index": jax.random.permutation(own_keys[7], STEPS).astype(jnp.int32),
        "step_gates": jnp.clip(jnp.exp(math.log(2.0) - 1.3862944 * jax.random.uniform(key_of[8], (STEPS, HEADS * HD), jnp.float32) ** block_levels(key_of[8], (STEPS, HEADS * HD), ((1, 2),), -0.2, 0.2)), 0.5, 2.0).astype(jnp.bfloat16),
    }


def angles(positions):
    pair_count = HD // 2
    side_pairs = HD // 6
    frame_pairs = pair_count - 2 * side_pairs
    position = positions.astype(jnp.int32)
    frame_index = (position // (GRID_H * GRID_W)).astype(jnp.float32)
    row_index = (position // GRID_W % GRID_H).astype(jnp.float32)
    column_index = (position % GRID_W).astype(jnp.float32)

    def frequencies(count):
        return jnp.exp(-math.log(10000.0) * jnp.arange(count, dtype=jnp.float32) / count)
    phases = jnp.concatenate([frame_index[:, None] * frequencies(frame_pairs)[None, :], row_index[:, None] * frequencies(side_pairs)[None, :], column_index[:, None] * frequencies(side_pairs)[None, :]], axis=1)
    return (jnp.cos(phases), jnp.sin(phases))

def rotate(source, cosine, sine):
    leading = source.shape[:-1]
    head_count = source.shape[-1] // HD
    paired = source.astype(jnp.float32).reshape(leading + (head_count, HD // 2, 2))
    real_part = paired[..., 0]
    imag_part = paired[..., 1]
    cos_part = cosine[:, None, :]
    sin_part = sine[:, None, :]
    turned = jnp.stack([real_part * cos_part - imag_part * sin_part, real_part * sin_part + imag_part * cos_part], axis=-1)
    return turned.reshape(source.shape)

def reference(queries, key_now, value_now, key_stale, value_stale, positions, exponents, step_index, step_gates):
    cosine, sine = angles(positions)
    query_turned = rotate(queries, cosine, sine).astype(jnp.bfloat16)
    key_turned = rotate(key_now, cosine, sine).astype(jnp.bfloat16)
    powers = jnp.repeat(jnp.exp2(exponents.astype(jnp.float32)), BLOCK, axis=2)
    head_shape = (2, TOKENS, HEADS, HD)

    def encode(current, stale, scaling):
        stale_wide = stale.astype(jnp.float32).reshape(head_shape)
        difference = (current.astype(jnp.float32).reshape(head_shape) - stale_wide) / scaling[..., None]
        sent = jnp.clip(difference, -448.0, 448.0).astype(jnp.bfloat16)
        return stale_wide + scaling[..., None] * sent.astype(jnp.float32)
    key_rebuilt = encode(key_turned, key_stale, powers[0])
    value_rebuilt = encode(value_now, value_stale, powers[1])
    query_wide = query_turned.astype(jnp.float32).reshape(head_shape)

    def by_head(array):
        return array.transpose(0, 2, 1, 3).reshape(2 * HEADS, TOKENS, HD)
    score_scale = 1.0 / math.sqrt(HD)

    def attend(triple):
        query_rows, key_rows, value_rows = triple
        scores = jnp.dot(query_rows, key_rows.T, precision=lax.Precision.HIGHEST) * score_scale
        peak_score = lax.optimization_barrier(jnp.max(scores, axis=1, keepdims=True))
        weights = jnp.exp(scores - peak_score).astype(jnp.bfloat16).astype(jnp.float32)
        weight_total = lax.optimization_barrier(jnp.sum(weights, axis=1, keepdims=True))
        return jnp.dot(weights, value_rows, precision=lax.Precision.HIGHEST) / weight_total
    mixture = lax.map(attend, (by_head(query_wide), by_head(key_rebuilt), by_head(value_rebuilt)))
    mixture = mixture.reshape(2, HEADS, TOKENS, HD).transpose(0, 2, 1, 3).reshape(2, TOKENS, HEADS * HD)
    gate_row = lax.dynamic_index_in_dim(step_gates, step_index[0], 0, keepdims=False).astype(jnp.float32)
    return (mixture * gate_row[None, None, :]).astype(jnp.bfloat16)
```

```python
import functools
import math

import jax
import jax.numpy as jnp
from jax import lax
from jax.experimental import pallas as pl
from jax.experimental.pallas import tpu as pltpu
from jax.sharding import PartitionSpec as P

HD = 128
BLOCK = 32
GRID_H = 16
GRID_W = 16
MESH = pl.DeviceIdType.MESH


def angles(positions):
    pair_count = HD // 2
    side_pairs = HD // 6
    frame_pairs = pair_count - 2 * side_pairs
    frame_index = (positions // (GRID_H * GRID_W)).astype(jnp.float32)
    row_index = (positions // GRID_W % GRID_H).astype(jnp.float32)
    column_index = (positions % GRID_W).astype(jnp.float32)

    def frequencies(count):
        return jnp.exp(-math.log(10000.0) * jnp.arange(count, dtype=jnp.float32) / count)

    phases = jnp.concatenate(
        [
            frame_index[:, None] * frequencies(frame_pairs)[None, :],
            row_index[:, None] * frequencies(side_pairs)[None, :],
            column_index[:, None] * frequencies(side_pairs)[None, :],
        ],
        axis=1,
    )
    return (jnp.cos(phases), jnp.sin(phases))


def rotate(source, cosine, sine):
    leading = source.shape[:-1]
    head_count = source.shape[-1] // HD
    paired = source.astype(jnp.float32).reshape(leading + (head_count, HD // 2, 2))
    real_part = paired[..., 0]
    imag_part = paired[..., 1]
    cos_part = cosine[:, None, :]
    sin_part = sine[:, None, :]
    turned = jnp.stack(
        [real_part * cos_part - imag_part * sin_part, real_part * sin_part + imag_part * cos_part],
        axis=-1,
    )
    return turned.reshape(source.shape)


def shards(
    queries,
    key_now,
    value_now,
    key_stale,
    value_stale,
    positions,
    exponents,
    step_index,
    step_gates,
):
    cosine, sine = angles(positions)
    query_turned = rotate(queries[0], cosine, sine).astype(jnp.bfloat16)
    key_turned = rotate(key_now[0], cosine, sine).astype(jnp.bfloat16)
    query_local, key_local, value_local = (
        lax.all_to_all(query_turned, "ulysses", split_axis=1, concat_axis=0, tiled=True),
        lax.all_to_all(key_turned, "ulysses", split_axis=1, concat_axis=0, tiled=True),
        lax.all_to_all(value_now[0], "ulysses", split_axis=1, concat_axis=0, tiled=True),
    )
    tok_rows = query_local.shape[0]
    feature_width = query_local.shape[1]
    head_count = feature_width // HD
    all_rows = key_stale.shape[1]
    first_row = lax.axis_index("blk") * tok_rows
    powers = jnp.repeat(jnp.exp2(exponents[:, 0].astype(jnp.float32)), BLOCK, axis=1)
    inverses = jnp.repeat(jnp.exp2(-exponents[:, 0].astype(jnp.float32)), BLOCK, axis=1)
    stale_keys = key_stale[0]
    stale_values = value_stale[0]

    def encode(current, stale, inverse):
        own_stale = lax.dynamic_slice_in_dim(stale, first_row, tok_rows, 0).astype(jnp.float32)
        own_inverse = lax.dynamic_slice_in_dim(inverse, first_row, tok_rows, 0)
        difference = (
            current.astype(jnp.float32).reshape(tok_rows, head_count, HD)
            - own_stale.reshape(tok_rows, head_count, HD)
        ) * own_inverse[:, :, None]
        return (
            jnp.clip(difference, -448.0, 448.0)
            .astype(jnp.bfloat16)
            .reshape(tok_rows, feature_width)
        )

    key_sent = encode(key_local, stale_keys, inverses[0])
    value_sent = encode(value_local, stale_values, inverses[1])
    query_heads = query_local.reshape(tok_rows, head_count, HD)
    score_scale = 1.0 / math.sqrt(HD)
    stale_scores = jnp.einsum(
        "qhd,khd->hqk",
        query_heads,
        stale_keys.reshape(all_rows, head_count, HD),
        preferred_element_type=jnp.float32,
    )
    key_whole, value_whole = (
        lax.all_gather(key_sent, "blk", axis=0, tiled=True),
        lax.all_gather(value_sent, "blk", axis=0, tiled=True),
    )
    span_rows = key_whole.shape[0]
    scaling = powers[0]
    residual = key_whole.reshape(span_rows, head_count, HD)
    scaled = (residual.astype(jnp.float32) * scaling[:, :, None]).astype(jnp.bfloat16)
    fresh_scores = jnp.einsum(
        "qhd,khd->hqk", query_heads, scaled, preferred_element_type=jnp.float32
    )
    scores = (stale_scores + fresh_scores) * score_scale
    peak_score = jnp.max(scores, axis=2, keepdims=True)
    weights = jnp.exp(scores - peak_score).astype(jnp.bfloat16)
    weight_total = jnp.sum(weights.astype(jnp.float32), axis=2)
    stale_sums = jnp.einsum(
        "hqk,khd->qhd",
        weights,
        stale_values.reshape(all_rows, head_count, HD),
        preferred_element_type=jnp.float32,
    )
    span_rows = value_whole.shape[0]
    scaling = powers[1]
    residual = value_whole.reshape(span_rows, head_count, HD)
    scaled = (residual.astype(jnp.float32) * scaling[:, :, None]).astype(jnp.bfloat16)
    fresh_sums = jnp.einsum("hqk,khd->qhd", weights, scaled, preferred_element_type=jnp.float32)
    mixture = (stale_sums + fresh_sums) / weight_total.T[:, :, None]
    gate_row = lax.dynamic_index_in_dim(step_gates, step_index[0], 0, keepdims=False).astype(
        jnp.float32
    )
    gated = (mixture * gate_row.reshape(head_count, HD)[None, :, :]).astype(jnp.bfloat16)
    restored = lax.all_to_all(
        gated.reshape(tok_rows, feature_width), "ulysses", split_axis=0, concat_axis=1, tiled=True
    )
    return restored[None]


def fused_kernel(
    nb,
    nu,
    q_ref,
    k_ref,
    v_ref,
    ks_ref,
    vs_ref,
    pos_ref,
    exp_ref,
    step_ref,
    gates_ref,
    out_ref,
    qkv_in,
    send,
    recv,
    stale,
    gates,
    mixed,
    in_sem,
    own_sem,
    fwd_send,
    fwd_recv,
    ret_send,
    ret_recv,
):
    rows = q_ref.shape[1]
    tokens = ks_ref.shape[1]
    blocks = exp_ref.shape[2]
    block = tokens // blocks
    peers = nb * nu
    own = send.shape[1]
    width = own * HD
    b = lax.axis_index("blk")
    u = lax.axis_index("ulysses")
    rank = u * nb + b
    offsets = [(db, du) for db in range(nb) for du in range(nu) if (db, du) != (0, 0)]
    offsets.sort(key=lambda pair: (-min(pair[0], nb - pair[0]), -pair[1]))

    def ahead(db, du):
        return lax.rem(b + db, nb), lax.rem(u + du, nu)

    def behind(db, du):
        return lax.rem(b + nb - db, nb), lax.rem(u + nu - du, nu)

    def token_rows(bb, uu):
        return pl.ds(pl.multiple_of((bb * nu + uu) * rows, rows), rows)

    barrier = pltpu.get_barrier_semaphore()
    for db, du in offsets:
        bb, uu = ahead(db, du)
        pl.semaphore_signal(
            barrier, inc=1, device_id={"blk": bb, "ulysses": uu}, device_id_type=MESH
        )

    columns = pl.ds(pl.multiple_of(b * width, width), width)
    loads = [
        pltpu.make_async_copy(k_ref.at[0], qkv_in.at[1], in_sem.at[1]),
        pltpu.make_async_copy(q_ref.at[0], qkv_in.at[0], in_sem.at[0]),
        pltpu.make_async_copy(v_ref.at[0], qkv_in.at[2], in_sem.at[2]),
        pltpu.make_async_copy(ks_ref.at[0, :, columns], stale.at[0], in_sem.at[3]),
        pltpu.make_async_copy(vs_ref.at[0, :, columns], stale.at[1], in_sem.at[4]),
        pltpu.make_async_copy(gates_ref.at[:, columns], gates, in_sem.at[5]),
    ]
    for load in loads:
        load.start()

    side = HD // 6
    front = HD // 2 - 2 * side
    lane = lax.broadcasted_iota(jnp.int32, (rows, HD), 1)
    row = lax.broadcasted_iota(jnp.int32, (rows, HD), 0)
    pair = lane >> 1
    even = (lane & 1) == 0
    position = jnp.zeros((rows, HD), jnp.int32)
    for t in range(rows):
        position = jnp.where(row == t, pos_ref[t], position)
    in_front = pair < front
    in_rows = pair < front + side
    place = jnp.where(
        in_front,
        position // (GRID_H * GRID_W),
        jnp.where(in_rows, position // GRID_W % GRID_H, position % GRID_W),
    ).astype(jnp.float32)
    within = jnp.where(in_front, pair, jnp.where(in_rows, pair - front, pair - front - side))
    count = jnp.where(in_front, float(front), float(side))
    phase = place * jnp.exp(-math.log(10000.0) * within.astype(jnp.float32) / count)
    cosine = jnp.cos(phase)
    sine = jnp.sin(phase)
    sine = jnp.where(even, -sine, sine)

    for load in loads[:3]:
        load.wait()
    for head in range(peers * own):
        to, j = divmod(head, own)
        at = slice(head * HD, (head + 1) * HD)
        for which in range(2):
            x = qkv_in[which, :, at].astype(jnp.float32)
            other = jnp.where(even, pltpu.roll(x, HD - 1, 1), pltpu.roll(x, 1, 1))
            send[to, j, which] = (x * cosine + other * sine).astype(jnp.bfloat16)
        send[to, j, 2] = qkv_in[2, :, at]

    pl.semaphore_wait(barrier, len(offsets))

    forward = []
    for j in range(own):
        for i, (db, du) in enumerate(offsets):
            bb, uu = ahead(db, du)
            copy = pltpu.make_async_remote_copy(
                src_ref=send.at[uu * nb + bb, j],
                dst_ref=recv.at[j, :, token_rows(b, u)],
                send_sem=fwd_send.at[j, i],
                recv_sem=fwd_recv.at[j, i],
                device_id={"blk": bb, "ulysses": uu},
                device_id_type=MESH,
            )
            copy.start()
            forward.append(copy)

    for j in range(own):
        recv[j, :, token_rows(b, u)] = send[rank, j]

    for load in loads[3:]:
        load.wait()
    chosen = lax.broadcasted_iota(jnp.int32, gates.shape, 0) == step_ref[0]
    gate_row = jnp.sum(
        jnp.where(chosen, gates[...].astype(jnp.float32), 0.0), axis=0, keepdims=True
    )

    def residual(which, j):
        at = slice(j * HD, (j + 1) * HD)
        parts = []
        for n in range(blocks):
            span = slice(n * block, (n + 1) * block)
            exponent = jnp.full((block, HD), exp_ref[which, 0, n, b * own + j], jnp.int32)
            one = jnp.ones_like(exponent)
            inverse = lax.shift_left(one, -exponent).astype(jnp.float32)
            power = lax.shift_left(one, exponent + 16).astype(jnp.float32) * 2.0**-16
            now = recv[j, 1 + which, span].astype(jnp.float32)
            before = stale[which, span, at].astype(jnp.float32)
            sent = jnp.clip((now - before) * inverse, -448.0, 448.0).astype(jnp.bfloat16)
            parts.append((sent.astype(jnp.float32) * power).astype(jnp.bfloat16))
        return jnp.concatenate(parts, axis=0)

    back = []
    for j in range(own):
        for i, (db, du) in enumerate(offsets):
            bb, uu = behind(db, du)
            pltpu.make_async_remote_copy(
                src_ref=send.at[rank, j],
                dst_ref=recv.at[j, :, token_rows(bb, uu)],
                send_sem=fwd_send.at[j, i],
                recv_sem=fwd_recv.at[j, i],
                device_id={"blk": bb, "ulysses": uu},
                device_id_type=MESH,
            ).wait_recv()
        at = slice(j * HD, (j + 1) * HD)
        query = recv[j, 0]
        keys = jnp.concatenate([stale[0, :, at], residual(0, j)], axis=1)
        scores = lax.dot_general(
            jnp.concatenate([query, query], axis=1),
            keys,
            (((1,), (1,)), ((), ())),
            preferred_element_type=jnp.float32,
        ) * (1.0 / math.sqrt(HD))
        peak = jnp.max(scores, axis=1, keepdims=True)
        weights = jnp.exp(scores - peak).astype(jnp.bfloat16)
        total = jnp.sum(weights.astype(jnp.float32), axis=1, keepdims=True)
        values = jnp.concatenate([stale[1, :, at], residual(1, j)], axis=0)
        sums = jnp.dot(
            jnp.concatenate([weights, weights], axis=1),
            values,
            preferred_element_type=jnp.float32,
        )
        mixed[j] = (sums / total * gate_row[:, at]).astype(jnp.bfloat16)
        target = pl.ds(pl.multiple_of((rank * own + j) * HD, HD), HD)
        for i, (db, du) in enumerate(offsets):
            bb, uu = ahead(db, du)
            copy = pltpu.make_async_remote_copy(
                src_ref=mixed.at[j, token_rows(bb, uu)],
                dst_ref=out_ref.at[0, :, target],
                send_sem=ret_send.at[j, i],
                recv_sem=ret_recv.at[j, i],
                device_id={"blk": bb, "ulysses": uu},
                device_id_type=MESH,
            )
            copy.start()
            back.append(copy)
        out_ref[0, :, target] = mixed[j, token_rows(b, u)]

    for copy in forward:
        copy.wait_send()
    for j in range(own):
        for i, (db, du) in enumerate(offsets):
            bb, uu = behind(db, du)
            source = (uu * nb + bb) * own + j
            pltpu.make_async_remote_copy(
                src_ref=mixed.at[j, token_rows(b, u)],
                dst_ref=out_ref.at[0, :, pl.ds(pl.multiple_of(source * HD, HD), HD)],
                send_sem=ret_send.at[j, i],
                recv_sem=ret_recv.at[j, i],
                device_id={"blk": bb, "ulysses": uu},
                device_id_type=MESH,
            ).wait_recv()
    for copy in back:
        copy.wait_send()


def fused(nb, nu, *args):
    queries, key_stale, step_gates = args[0], args[3], args[8]
    rows, features = queries.shape[1:]
    tokens, columns = key_stale.shape[1:]
    own = columns // HD // nb
    width = own * HD
    peers = nb * nu
    hbm = pl.BlockSpec(memory_space=pl.ANY)
    smem = pl.BlockSpec(memory_space=pltpu.SMEM)
    pairs = pltpu.SemaphoreType.DMA((own, peers - 1))
    return pl.pallas_call(
        functools.partial(fused_kernel, nb, nu),
        out_shape=jax.ShapeDtypeStruct(queries.shape, jnp.bfloat16),
        in_specs=[hbm] * 5 + [smem] * 3 + [hbm],
        out_specs=pl.BlockSpec(memory_space=pltpu.VMEM),
        scratch_shapes=[
            pltpu.VMEM((3, rows, features), jnp.bfloat16),
            pltpu.VMEM((peers, own, 3, rows, HD), jnp.bfloat16),
            pltpu.VMEM((own, 3, tokens, HD), jnp.bfloat16),
            pltpu.VMEM((2, tokens, width), jnp.bfloat16),
            pltpu.VMEM((step_gates.shape[0], width), jnp.bfloat16),
            pltpu.VMEM((own, tokens, HD), jnp.bfloat16),
            pltpu.SemaphoreType.DMA((6,)),
            pltpu.SemaphoreType.DMA,
            pairs,
            pairs,
            pairs,
            pairs,
        ],
        compiler_params=pltpu.CompilerParams(collective_id=0, has_side_effects=True),
    )(*args)


def solution(mesh):
    nb, nu = mesh.shape["blk"], mesh.shape["ulysses"]

    def body(*args):
        heads = args[3].shape[2] // HD
        if heads % nb == 0 and nb * nu > 1:
            return fused(nb, nu, *args)
        return shards(*args)

    return jax.shard_map(
        body,
        mesh=mesh,
        in_specs=(
            P("cfg", ("groups", "blk", "ulysses"), None),
            P("cfg", ("groups", "blk", "ulysses"), None),
            P("cfg", ("groups", "blk", "ulysses"), None),
            P("cfg", "groups", "ulysses"),
            P("cfg", "groups", "ulysses"),
            P(("groups", "blk", "ulysses")),
            P(None, "cfg", "groups", "ulysses"),
            P("groups"),
            P(None, "ulysses"),
        ),
        out_specs=P("cfg", ("groups", "blk", "ulysses"), None),
        check_vma=False,
    )
```

```python
import functools
import math

import jax
import jax.numpy as jnp
from jax import lax
from jax.experimental import pallas as pl
from jax.experimental.pallas import tpu as pltpu
from jax.sharding import PartitionSpec as P

HD = 128
BLOCK = 32
GRID_H = 16
GRID_W = 16
MESH = pl.DeviceIdType.MESH


def angles(positions):
    pair_count = HD // 2
    side_pairs = HD // 6
    frame_pairs = pair_count - 2 * side_pairs
    frame_index = (positions // (GRID_H * GRID_W)).astype(jnp.float32)
    row_index = (positions // GRID_W % GRID_H).astype(jnp.float32)
    column_index = (positions % GRID_W).astype(jnp.float32)

    def frequencies(count):
        return jnp.exp(-math.log(10000.0) * jnp.arange(count, dtype=jnp.float32) / count)

    phases = jnp.concatenate(
        [
            frame_index[:, None] * frequencies(frame_pairs)[None, :],
            row_index[:, None] * frequencies(side_pairs)[None, :],
            column_index[:, None] * frequencies(side_pairs)[None, :],
        ],
        axis=1,
    )
    return (jnp.cos(phases), jnp.sin(phases))


def rotate(source, cosine, sine):
    leading = source.shape[:-1]
    head_count = source.shape[-1] // HD
    paired = source.astype(jnp.float32).reshape(leading + (head_count, HD // 2, 2))
    real_part = paired[..., 0]
    imag_part = paired[..., 1]
    cos_part = cosine[:, None, :]
    sin_part = sine[:, None, :]
    turned = jnp.stack(
        [real_part * cos_part - imag_part * sin_part, real_part * sin_part + imag_part * cos_part],
        axis=-1,
    )
    return turned.reshape(source.shape)


def shards(
    queries,
    key_now,
    value_now,
    key_stale,
    value_stale,
    positions,
    exponents,
    step_index,
    step_gates,
):
    cosine, sine = angles(positions)
    query_turned = rotate(queries[0], cosine, sine).astype(jnp.bfloat16)
    key_turned = rotate(key_now[0], cosine, sine).astype(jnp.bfloat16)
    query_local, key_local, value_local = (
        lax.all_to_all(query_turned, "ulysses", split_axis=1, concat_axis=0, tiled=True),
        lax.all_to_all(key_turned, "ulysses", split_axis=1, concat_axis=0, tiled=True),
        lax.all_to_all(value_now[0], "ulysses", split_axis=1, concat_axis=0, tiled=True),
    )
    tok_rows = query_local.shape[0]
    feature_width = query_local.shape[1]
    head_count = feature_width // HD
    all_rows = key_stale.shape[1]
    first_row = lax.axis_index("blk") * tok_rows
    powers = jnp.repeat(jnp.exp2(exponents[:, 0].astype(jnp.float32)), BLOCK, axis=1)
    inverses = jnp.repeat(jnp.exp2(-exponents[:, 0].astype(jnp.float32)), BLOCK, axis=1)
    stale_keys = key_stale[0]
    stale_values = value_stale[0]

    def encode(current, stale, inverse):
        own_stale = lax.dynamic_slice_in_dim(stale, first_row, tok_rows, 0).astype(jnp.float32)
        own_inverse = lax.dynamic_slice_in_dim(inverse, first_row, tok_rows, 0)
        difference = (
            current.astype(jnp.float32).reshape(tok_rows, head_count, HD)
            - own_stale.reshape(tok_rows, head_count, HD)
        ) * own_inverse[:, :, None]
        return (
            jnp.clip(difference, -448.0, 448.0)
            .astype(jnp.bfloat16)
            .reshape(tok_rows, feature_width)
        )

    key_sent = encode(key_local, stale_keys, inverses[0])
    value_sent = encode(value_local, stale_values, inverses[1])
    query_heads = query_local.reshape(tok_rows, head_count, HD)
    score_scale = 1.0 / math.sqrt(HD)
    stale_scores = jnp.einsum(
        "qhd,khd->hqk",
        query_heads,
        stale_keys.reshape(all_rows, head_count, HD),
        preferred_element_type=jnp.float32,
    )
    key_whole, value_whole = (
        lax.all_gather(key_sent, "blk", axis=0, tiled=True),
        lax.all_gather(value_sent, "blk", axis=0, tiled=True),
    )
    span_rows = key_whole.shape[0]
    scaling = powers[0]
    residual = key_whole.reshape(span_rows, head_count, HD)
    scaled = (residual.astype(jnp.float32) * scaling[:, :, None]).astype(jnp.bfloat16)
    fresh_scores = jnp.einsum(
        "qhd,khd->hqk", query_heads, scaled, preferred_element_type=jnp.float32
    )
    scores = (stale_scores + fresh_scores) * score_scale
    peak_score = jnp.max(scores, axis=2, keepdims=True)
    weights = jnp.exp(scores - peak_score).astype(jnp.bfloat16)
    weight_total = jnp.sum(weights.astype(jnp.float32), axis=2)
    stale_sums = jnp.einsum(
        "hqk,khd->qhd",
        weights,
        stale_values.reshape(all_rows, head_count, HD),
        preferred_element_type=jnp.float32,
    )
    span_rows = value_whole.shape[0]
    scaling = powers[1]
    residual = value_whole.reshape(span_rows, head_count, HD)
    scaled = (residual.astype(jnp.float32) * scaling[:, :, None]).astype(jnp.bfloat16)
    fresh_sums = jnp.einsum("hqk,khd->qhd", weights, scaled, preferred_element_type=jnp.float32)
    mixture = (stale_sums + fresh_sums) / weight_total.T[:, :, None]
    gate_row = lax.dynamic_index_in_dim(step_gates, step_index[0], 0, keepdims=False).astype(
        jnp.float32
    )
    gated = (mixture * gate_row.reshape(head_count, HD)[None, :, :]).astype(jnp.bfloat16)
    restored = lax.all_to_all(
        gated.reshape(tok_rows, feature_width), "ulysses", split_axis=0, concat_axis=1, tiled=True
    )
    return restored[None]


def fused_kernel(
    nb,
    nu,
    q_ref,
    k_ref,
    v_ref,
    ks_ref,
    vs_ref,
    pos_hbm,
    exp_hbm,
    step_hbm,
    gates_ref,
    out_ref,
    qkv_in,
    send,
    recv,
    stale,
    gates,
    mixed,
    pos_ref,
    exp_ref,
    step_ref,
    in_sem,
    fwd_send,
    fwd_recv,
    ret_send,
    ret_recv,
):
    rows = q_ref.shape[1]
    tokens = ks_ref.shape[1]
    blocks = exp_ref.shape[2]
    block = tokens // blocks
    own = send.shape[1]
    width = own * HD
    b = lax.axis_index("blk")
    u = lax.axis_index("ulysses")
    rank = u * nb + b
    place_of = b * nu + u
    offsets = [(db, du) for db in range(nb) for du in range(nu) if (db, du) != (0, 0)]
    offsets.sort(key=lambda pair: (-min(pair[0], nb - pair[0]), -pair[1]))

    def ahead(db, du):
        return lax.rem(b + db, nb), lax.rem(u + du, nu)

    def behind(db, du):
        return lax.rem(b + nb - db, nb), lax.rem(u + nu - du, nu)

    def token_rows(bb, uu):
        return pl.ds(pl.multiple_of((bb * nu + uu) * rows, rows), rows)

    def head_columns(of_rank):
        return pl.ds(pl.multiple_of(of_rank * width, width), width)

    barrier = pltpu.get_barrier_semaphore()
    for db, du in offsets:
        bb, uu = ahead(db, du)
        pl.semaphore_signal(
            barrier, inc=1, device_id={"blk": bb, "ulysses": uu}, device_id_type=MESH
        )

    columns = head_columns(b)
    loads = [
        pltpu.make_async_copy(pos_hbm, pos_ref, in_sem.at[0]),
        pltpu.make_async_copy(q_ref.at[0], qkv_in.at[0], in_sem.at[1]),
        pltpu.make_async_copy(k_ref.at[0], qkv_in.at[1], in_sem.at[2]),
        pltpu.make_async_copy(v_ref.at[0], qkv_in.at[2], in_sem.at[3]),
        pltpu.make_async_copy(exp_hbm, exp_ref, in_sem.at[4]),
        pltpu.make_async_copy(step_hbm, step_ref, in_sem.at[5]),
        pltpu.make_async_copy(ks_ref.at[0, :, columns], stale.at[0], in_sem.at[6]),
        pltpu.make_async_copy(vs_ref.at[0, :, columns], stale.at[1], in_sem.at[7]),
        pltpu.make_async_copy(gates_ref.at[:, columns], gates, in_sem.at[8]),
    ]
    for load in loads:
        load.start()

    side = HD // 6
    front = HD // 2 - 2 * side
    lane = lax.broadcasted_iota(jnp.int32, (rows, HD), 1)
    row = lax.broadcasted_iota(jnp.int32, (rows, HD), 0)
    pair = lane >> 1
    even = (lane & 1) == 0
    in_front = pair < front
    in_rows = pair < front + side
    within = jnp.where(in_front, pair, jnp.where(in_rows, pair - front, pair - front - side))
    count = jnp.where(in_front, float(front), float(side))
    frequency = jnp.exp(-math.log(10000.0) * within.astype(jnp.float32) / count)
    loads[0].wait()
    position = jnp.zeros((rows, HD), jnp.int32)
    for t in range(rows):
        position = jnp.where(row == t, pos_ref[t], position)
    place = jnp.where(
        in_front,
        position // (GRID_H * GRID_W),
        jnp.where(in_rows, position // GRID_W % GRID_H, position % GRID_W),
    ).astype(jnp.float32)
    phase = place * frequency
    cosine = jnp.cos(phase)
    sine = jnp.sin(phase)
    sine = jnp.where(even, -sine, sine)

    for load in loads[1:4]:
        load.wait()

    def turned(which, head):
        x = qkv_in[which, :, pl.ds(pl.multiple_of(head * HD, HD), HD)].astype(jnp.float32)
        other = jnp.where(even, pltpu.roll(x, HD - 1, 1), pltpu.roll(x, 1, 1))
        return (x * cosine + other * sine).astype(jnp.bfloat16)

    def fill(target, to_rank):
        for j in range(own):
            head = to_rank * own + j
            target[j, 0] = turned(0, head)
            target[j, 1] = turned(1, head)
            target[j, 2] = qkv_in[2, :, pl.ds(pl.multiple_of(head * HD, HD), HD)]

    def forward(i, db, du):
        bb, uu = ahead(db, du)
        return pltpu.make_async_remote_copy(
            src_ref=send.at[i],
            dst_ref=recv.at[place_of],
            send_sem=fwd_send.at[i],
            recv_sem=fwd_recv.at[i],
            device_id={"blk": bb, "ulysses": uu},
            device_id_type=MESH,
        )

    for i, (db, du) in enumerate(offsets):
        bb, uu = ahead(db, du)
        fill(send.at[i], uu * nb + bb)
        if i == 0:
            pl.semaphore_wait(barrier, len(offsets))
        forward(i, db, du).start()
    fill(recv.at[place_of], rank)

    for load in loads[4:]:
        load.wait()
    chosen = lax.broadcasted_iota(jnp.int32, gates.shape, 0) == step_ref[0]
    gate_row = jnp.sum(
        jnp.where(chosen, gates[...].astype(jnp.float32), 0.0), axis=0, keepdims=True
    )

    def residual(which, j):
        at = slice(j * HD, (j + 1) * HD)
        parts = []
        per = block // rows
        for n in range(blocks):
            span = slice(n * block, (n + 1) * block)
            exponent = jnp.full((block, HD), exp_ref[which, 0, n, b * own + j], jnp.int32)
            one = jnp.ones_like(exponent)
            inverse = lax.shift_left(one, -exponent).astype(jnp.float32)
            power = lax.shift_left(one, exponent + 16).astype(jnp.float32) * 2.0**-16
            now = jnp.concatenate(
                [recv[n * per + m, j, 1 + which] for m in range(per)], axis=0
            ).astype(jnp.float32)
            before = stale[which, span, at].astype(jnp.float32)
            sent = jnp.clip((now - before) * inverse, -448.0, 448.0).astype(jnp.bfloat16)
            parts.append((sent.astype(jnp.float32) * power).astype(jnp.bfloat16))
        return jnp.concatenate(parts, axis=0)

    for i, (db, du) in enumerate(offsets):
        bb, uu = behind(db, du)
        pltpu.make_async_remote_copy(
            src_ref=send.at[i],
            dst_ref=recv.at[bb * nu + uu],
            send_sem=fwd_send.at[i],
            recv_sem=fwd_recv.at[i],
            device_id={"blk": bb, "ulysses": uu},
            device_id_type=MESH,
        ).wait_recv()

    for j in range(own):
        at = slice(j * HD, (j + 1) * HD)
        query = jnp.concatenate([recv[t, j, 0] for t in range(nb * nu)], axis=0)
        keys = jnp.concatenate([stale[0, :, at], residual(0, j)], axis=1)
        scores = lax.dot_general(
            jnp.concatenate([query, query], axis=1),
            keys,
            (((1,), (1,)), ((), ())),
            preferred_element_type=jnp.float32,
        ) * (1.0 / math.sqrt(HD))
        peak = jnp.max(scores, axis=1, keepdims=True)
        weights = jnp.exp(scores - peak).astype(jnp.bfloat16)
        total = jnp.sum(weights.astype(jnp.float32), axis=1, keepdims=True)
        values = jnp.concatenate([stale[1, :, at], residual(1, j)], axis=0)
        sums = jnp.dot(
            jnp.concatenate([weights, weights], axis=1),
            values,
            preferred_element_type=jnp.float32,
        )
        mixed[:, at] = (sums / total * gate_row[:, at]).astype(jnp.bfloat16)

    def back(i, db, du):
        bb, uu = ahead(db, du)
        return pltpu.make_async_remote_copy(
            src_ref=mixed.at[token_rows(bb, uu)],
            dst_ref=out_ref.at[0, :, head_columns(rank)],
            send_sem=ret_send.at[i],
            recv_sem=ret_recv.at[i],
            device_id={"blk": bb, "ulysses": uu},
            device_id_type=MESH,
        )

    for i, (db, du) in enumerate(offsets):
        back(i, db, du).start()
    out_ref[0, :, head_columns(rank)] = mixed[token_rows(b, u)]
    for i, (db, du) in enumerate(offsets):
        forward(i, db, du).wait_send()
    for i, (db, du) in enumerate(offsets):
        bb, uu = behind(db, du)
        pltpu.make_async_remote_copy(
            src_ref=mixed.at[token_rows(b, u)],
            dst_ref=out_ref.at[0, :, head_columns(uu * nb + bb)],
            send_sem=ret_send.at[i],
            recv_sem=ret_recv.at[i],
            device_id={"blk": bb, "ulysses": uu},
            device_id_type=MESH,
        ).wait_recv()
    for i, (db, du) in enumerate(offsets):
        back(i, db, du).wait_send()


def fused(nb, nu, *args):
    queries, key_stale, positions, exponents, step_index, step_gates = (
        args[0],
        args[3],
        *args[5:],
    )
    rows, features = queries.shape[1:]
    tokens, columns = key_stale.shape[1:]
    own = columns // HD // nb
    width = own * HD
    peers = nb * nu
    hbm = pl.BlockSpec(memory_space=pl.ANY)
    pairs = pltpu.SemaphoreType.DMA((peers - 1,))
    return pl.pallas_call(
        functools.partial(fused_kernel, nb, nu),
        out_shape=jax.ShapeDtypeStruct(queries.shape, jnp.bfloat16),
        in_specs=[hbm] * 9,
        out_specs=pl.BlockSpec(memory_space=pltpu.VMEM),
        scratch_shapes=[
            pltpu.VMEM((3, rows, features), jnp.bfloat16),
            pltpu.VMEM((peers - 1, own, 3, rows, HD), jnp.bfloat16),
            pltpu.VMEM((peers, own, 3, rows, HD), jnp.bfloat16),
            pltpu.VMEM((2, tokens, width), jnp.bfloat16),
            pltpu.VMEM((step_gates.shape[0], width), jnp.bfloat16),
            pltpu.VMEM((tokens, width), jnp.bfloat16),
            pltpu.SMEM(positions.shape, jnp.int32),
            pltpu.SMEM(exponents.shape, jnp.int32),
            pltpu.SMEM(step_index.shape, jnp.int32),
            pltpu.SemaphoreType.DMA((9,)),
            pairs,
            pairs,
            pairs,
            pairs,
        ],
        compiler_params=pltpu.CompilerParams(collective_id=0, has_side_effects=True),
    )(*args)


def solution(mesh):
    nb, nu = mesh.shape["blk"], mesh.shape["ulysses"]

    def body(*args):
        heads = args[3].shape[2] // HD
        if heads % nb == 0 and nb * nu > 1:
            return fused(nb, nu, *args)
        return shards(*args)

    return jax.shard_map(
        body,
        mesh=mesh,
        in_specs=(
            P("cfg", ("groups", "blk", "ulysses"), None),
            P("cfg", ("groups", "blk", "ulysses"), None),
            P("cfg", ("groups", "blk", "ulysses"), None),
            P("cfg", "groups", "ulysses"),
            P("cfg", "groups", "ulysses"),
            P(("groups", "blk", "ulysses")),
            P(None, "cfg", "groups", "ulysses"),
            P("groups"),
            P(None, "ulysses"),
        ),
        out_specs=P("cfg", ("groups", "blk", "ulysses"), None),
        check_vma=False,
    )
```

```python
import functools
import math

import jax
import jax.numpy as jnp
from jax import lax
from jax.experimental import pallas as pl
from jax.experimental.pallas import tpu as pltpu
from jax.sharding import PartitionSpec as P

HD = 128
BLOCK = 32
GRID_H = 16
GRID_W = 16
MESH = pl.DeviceIdType.MESH


def angles(positions):
    pair_count = HD // 2
    side_pairs = HD // 6
    frame_pairs = pair_count - 2 * side_pairs
    frame_index = (positions // (GRID_H * GRID_W)).astype(jnp.float32)
    row_index = (positions // GRID_W % GRID_H).astype(jnp.float32)
    column_index = (positions % GRID_W).astype(jnp.float32)

    def frequencies(count):
        return jnp.exp(-math.log(10000.0) * jnp.arange(count, dtype=jnp.float32) / count)

    phases = jnp.concatenate(
        [
            frame_index[:, None] * frequencies(frame_pairs)[None, :],
            row_index[:, None] * frequencies(side_pairs)[None, :],
            column_index[:, None] * frequencies(side_pairs)[None, :],
        ],
        axis=1,
    )
    return (jnp.cos(phases), jnp.sin(phases))


def rotate(source, cosine, sine):
    leading = source.shape[:-1]
    head_count = source.shape[-1] // HD
    paired = source.astype(jnp.float32).reshape(leading + (head_count, HD // 2, 2))
    real_part = paired[..., 0]
    imag_part = paired[..., 1]
    cos_part = cosine[:, None, :]
    sin_part = sine[:, None, :]
    turned = jnp.stack(
        [real_part * cos_part - imag_part * sin_part, real_part * sin_part + imag_part * cos_part],
        axis=-1,
    )
    return turned.reshape(source.shape)


def shards(
    queries,
    key_now,
    value_now,
    key_stale,
    value_stale,
    positions,
    exponents,
    step_index,
    step_gates,
):
    cosine, sine = angles(positions)
    query_turned = rotate(queries[0], cosine, sine).astype(jnp.bfloat16)
    key_turned = rotate(key_now[0], cosine, sine).astype(jnp.bfloat16)
    query_local, key_local, value_local = (
        lax.all_to_all(query_turned, "ulysses", split_axis=1, concat_axis=0, tiled=True),
        lax.all_to_all(key_turned, "ulysses", split_axis=1, concat_axis=0, tiled=True),
        lax.all_to_all(value_now[0], "ulysses", split_axis=1, concat_axis=0, tiled=True),
    )
    tok_rows = query_local.shape[0]
    feature_width = query_local.shape[1]
    head_count = feature_width // HD
    all_rows = key_stale.shape[1]
    first_row = lax.axis_index("blk") * tok_rows
    powers = jnp.repeat(jnp.exp2(exponents[:, 0].astype(jnp.float32)), BLOCK, axis=1)
    inverses = jnp.repeat(jnp.exp2(-exponents[:, 0].astype(jnp.float32)), BLOCK, axis=1)
    stale_keys = key_stale[0]
    stale_values = value_stale[0]

    def encode(current, stale, inverse):
        own_stale = lax.dynamic_slice_in_dim(stale, first_row, tok_rows, 0).astype(jnp.float32)
        own_inverse = lax.dynamic_slice_in_dim(inverse, first_row, tok_rows, 0)
        difference = (
            current.astype(jnp.float32).reshape(tok_rows, head_count, HD)
            - own_stale.reshape(tok_rows, head_count, HD)
        ) * own_inverse[:, :, None]
        return (
            jnp.clip(difference, -448.0, 448.0)
            .astype(jnp.bfloat16)
            .reshape(tok_rows, feature_width)
        )

    key_sent = encode(key_local, stale_keys, inverses[0])
    value_sent = encode(value_local, stale_values, inverses[1])
    query_heads = query_local.reshape(tok_rows, head_count, HD)
    score_scale = 1.0 / math.sqrt(HD)
    stale_scores = jnp.einsum(
        "qhd,khd->hqk",
        query_heads,
        stale_keys.reshape(all_rows, head_count, HD),
        preferred_element_type=jnp.float32,
    )
    key_whole, value_whole = (
        lax.all_gather(key_sent, "blk", axis=0, tiled=True),
        lax.all_gather(value_sent, "blk", axis=0, tiled=True),
    )
    span_rows = key_whole.shape[0]
    scaling = powers[0]
    residual = key_whole.reshape(span_rows, head_count, HD)
    scaled = (residual.astype(jnp.float32) * scaling[:, :, None]).astype(jnp.bfloat16)
    fresh_scores = jnp.einsum(
        "qhd,khd->hqk", query_heads, scaled, preferred_element_type=jnp.float32
    )
    scores = (stale_scores + fresh_scores) * score_scale
    peak_score = jnp.max(scores, axis=2, keepdims=True)
    weights = jnp.exp(scores - peak_score).astype(jnp.bfloat16)
    weight_total = jnp.sum(weights.astype(jnp.float32), axis=2)
    stale_sums = jnp.einsum(
        "hqk,khd->qhd",
        weights,
        stale_values.reshape(all_rows, head_count, HD),
        preferred_element_type=jnp.float32,
    )
    span_rows = value_whole.shape[0]
    scaling = powers[1]
    residual = value_whole.reshape(span_rows, head_count, HD)
    scaled = (residual.astype(jnp.float32) * scaling[:, :, None]).astype(jnp.bfloat16)
    fresh_sums = jnp.einsum("hqk,khd->qhd", weights, scaled, preferred_element_type=jnp.float32)
    mixture = (stale_sums + fresh_sums) / weight_total.T[:, :, None]
    gate_row = lax.dynamic_index_in_dim(step_gates, step_index[0], 0, keepdims=False).astype(
        jnp.float32
    )
    gated = (mixture * gate_row.reshape(head_count, HD)[None, :, :]).astype(jnp.bfloat16)
    restored = lax.all_to_all(
        gated.reshape(tok_rows, feature_width), "ulysses", split_axis=0, concat_axis=1, tiled=True
    )
    return restored[None]


def fused_kernel(
    nb,
    nu,
    q_ref,
    k_ref,
    v_ref,
    ks_ref,
    vs_ref,
    pos_hbm,
    exp_hbm,
    step_hbm,
    gates_ref,
    out_ref,
    qkv_in,
    send,
    recv,
    stale,
    gates,
    mixed,
    pos_ref,
    exp_ref,
    step_ref,
    in_sem,
    fwd_send,
    fwd_recv,
    ret_send,
    ret_recv,
):
    rows = q_ref.shape[1]
    tokens = ks_ref.shape[1]
    blocks = exp_ref.shape[2]
    block = tokens // blocks
    own = send.shape[1]
    width = own * HD
    b = lax.axis_index("blk")
    u = lax.axis_index("ulysses")
    rank = u * nb + b
    place_of = b * nu + u
    offsets = [(db, du) for db in range(nb) for du in range(nu) if (db, du) != (0, 0)]
    offsets.sort(key=lambda pair: (-min(pair[0], nb - pair[0]), -pair[1]))

    def ahead(db, du):
        return lax.rem(b + db, nb), lax.rem(u + du, nu)

    def behind(db, du):
        return lax.rem(b + nb - db, nb), lax.rem(u + nu - du, nu)

    def token_rows(bb, uu):
        return pl.ds(pl.multiple_of((bb * nu + uu) * rows, rows), rows)

    def head_columns(of_rank):
        return pl.ds(pl.multiple_of(of_rank * width, width), width)

    barrier = pltpu.get_barrier_semaphore()
    for db, du in offsets:
        bb, uu = ahead(db, du)
        pl.semaphore_signal(
            barrier, inc=1, device_id={"blk": bb, "ulysses": uu}, device_id_type=MESH
        )

    columns = head_columns(b)
    loads = [
        pltpu.make_async_copy(pos_hbm, pos_ref, in_sem.at[0]),
        pltpu.make_async_copy(q_ref.at[0], qkv_in.at[0], in_sem.at[1]),
        pltpu.make_async_copy(k_ref.at[0], qkv_in.at[1], in_sem.at[2]),
        pltpu.make_async_copy(v_ref.at[0], qkv_in.at[2], in_sem.at[3]),
        pltpu.make_async_copy(exp_hbm, exp_ref, in_sem.at[4]),
        pltpu.make_async_copy(step_hbm, step_ref, in_sem.at[5]),
        pltpu.make_async_copy(ks_ref.at[0, :, columns], stale.at[0], in_sem.at[6]),
        pltpu.make_async_copy(vs_ref.at[0, :, columns], stale.at[1], in_sem.at[7]),
        pltpu.make_async_copy(gates_ref.at[:, columns], gates, in_sem.at[8]),
    ]
    for load in loads:
        load.start()

    side = HD // 6
    front = HD // 2 - 2 * side
    lane = lax.broadcasted_iota(jnp.int32, (rows, HD), 1)
    row = lax.broadcasted_iota(jnp.int32, (rows, HD), 0)
    pair = lane >> 1
    even = (lane & 1) == 0
    in_front = pair < front
    in_rows = pair < front + side
    within = jnp.where(in_front, pair, jnp.where(in_rows, pair - front, pair - front - side))
    count = jnp.where(in_front, float(front), float(side))
    frequency = jnp.exp(-math.log(10000.0) * within.astype(jnp.float32) / count)
    loads[0].wait()
    position = jnp.zeros((rows, HD), jnp.int32)
    for t in range(rows):
        position = jnp.where(row == t, pos_ref[t], position)
    place = jnp.where(
        in_front,
        position // (GRID_H * GRID_W),
        jnp.where(in_rows, position // GRID_W % GRID_H, position % GRID_W),
    ).astype(jnp.float32)
    phase = place * frequency
    cosine = jnp.cos(phase)
    sine = jnp.sin(phase)
    sine = jnp.where(even, -sine, sine)

    for load in loads[1:4]:
        load.wait()

    def turned(which, head):
        x = qkv_in[which, :, pl.ds(pl.multiple_of(head * HD, HD), HD)].astype(jnp.float32)
        other = jnp.where(even, pltpu.roll(x, HD - 1, 1), pltpu.roll(x, 1, 1))
        return (x * cosine + other * sine).astype(jnp.bfloat16)

    def fill(target, to_rank):
        for j in range(own):
            head = to_rank * own + j
            target[j, 0] = turned(0, head)
            target[j, 1] = turned(1, head)
            target[j, 2] = qkv_in[2, :, pl.ds(pl.multiple_of(head * HD, HD), HD)]

    def forward(i, db, du):
        bb, uu = ahead(db, du)
        return pltpu.make_async_remote_copy(
            src_ref=send.at[i],
            dst_ref=recv.at[place_of],
            send_sem=fwd_send.at[i],
            recv_sem=fwd_recv.at[i],
            device_id={"blk": bb, "ulysses": uu},
            device_id_type=MESH,
        )

    for i, (db, du) in enumerate(offsets):
        bb, uu = ahead(db, du)
        fill(send.at[i], uu * nb + bb)
        if i == 0:
            pl.semaphore_wait(barrier, len(offsets))
        forward(i, db, du).start()
    fill(recv.at[place_of], rank)

    for load in loads[4:]:
        load.wait()
    chosen = lax.broadcasted_iota(jnp.int32, gates.shape, 0) == step_ref[0]
    gate_row = jnp.sum(
        jnp.where(chosen, gates[...].astype(jnp.float32), 0.0), axis=0, keepdims=True
    )

    def residual(which, j):
        at = slice(j * HD, (j + 1) * HD)
        parts = []
        per = block // rows
        for n in range(blocks):
            span = slice(n * block, (n + 1) * block)
            exponent = jnp.full((block, HD), exp_ref[which, 0, n, b * own + j], jnp.int32)
            one = jnp.ones_like(exponent)
            inverse = lax.shift_left(one, -exponent).astype(jnp.float32)
            power = lax.shift_left(one, exponent + 16).astype(jnp.float32) * 2.0**-16
            now = jnp.concatenate(
                [recv[n * per + m, j, 1 + which] for m in range(per)], axis=0
            ).astype(jnp.float32)
            before = stale[which, span, at].astype(jnp.float32)
            sent = jnp.clip((now - before) * inverse, -448.0, 448.0).astype(jnp.bfloat16)
            parts.append((sent.astype(jnp.float32) * power).astype(jnp.bfloat16))
        return jnp.concatenate(parts, axis=0)

    for i, (db, du) in enumerate(offsets):
        bb, uu = behind(db, du)
        pltpu.make_async_remote_copy(
            src_ref=send.at[i],
            dst_ref=recv.at[bb * nu + uu],
            send_sem=fwd_send.at[i],
            recv_sem=fwd_recv.at[i],
            device_id={"blk": bb, "ulysses": uu},
            device_id_type=MESH,
        ).wait_recv()

    for j in range(own):
        at = slice(j * HD, (j + 1) * HD)
        query = jnp.concatenate([recv[t, j, 0] for t in range(nb * nu)], axis=0)
        keys = jnp.concatenate([stale[0, :, at], residual(0, j)], axis=1)
        scores = lax.dot_general(
            jnp.concatenate([query, query], axis=1),
            keys,
            (((1,), (1,)), ((), ())),
            preferred_element_type=jnp.float32,
        ) * (1.0 / math.sqrt(HD))
        peak = jnp.max(scores, axis=1, keepdims=True)
        weights = jnp.exp(scores - peak).astype(jnp.bfloat16)
        total = jnp.sum(weights.astype(jnp.float32), axis=1, keepdims=True)
        values = jnp.concatenate([stale[1, :, at], residual(1, j)], axis=0)
        sums = jnp.dot(
            jnp.concatenate([weights, weights], axis=1),
            values,
            preferred_element_type=jnp.float32,
        )
        mixed[:, at] = (sums / total * gate_row[:, at]).astype(jnp.bfloat16)

    def back(i, db, du):
        bb, uu = ahead(db, du)
        return pltpu.make_async_remote_copy(
            src_ref=mixed.at[token_rows(bb, uu)],
            dst_ref=out_ref.at[0, :, head_columns(rank)],
            send_sem=ret_send.at[i],
            recv_sem=ret_recv.at[i],
            device_id={"blk": bb, "ulysses": uu},
            device_id_type=MESH,
        )

    for i, (db, du) in enumerate(offsets):
        back(i, db, du).start()
    kept = pltpu.make_async_copy(
        mixed.at[token_rows(b, u)], out_ref.at[0, :, head_columns(rank)], in_sem.at[9]
    )
    kept.start()
    for i, (db, du) in enumerate(offsets):
        forward(i, db, du).wait_send()
    for i, (db, du) in enumerate(offsets):
        bb, uu = behind(db, du)
        pltpu.make_async_remote_copy(
            src_ref=mixed.at[token_rows(b, u)],
            dst_ref=out_ref.at[0, :, head_columns(uu * nb + bb)],
            send_sem=ret_send.at[i],
            recv_sem=ret_recv.at[i],
            device_id={"blk": bb, "ulysses": uu},
            device_id_type=MESH,
        ).wait_recv()
    for i, (db, du) in enumerate(offsets):
        back(i, db, du).wait_send()
    kept.wait()


def fused(nb, nu, *args):
    queries, key_stale, positions, exponents, step_index, step_gates = (
        args[0],
        args[3],
        *args[5:],
    )
    rows, features = queries.shape[1:]
    tokens, columns = key_stale.shape[1:]
    own = columns // HD // nb
    width = own * HD
    peers = nb * nu
    hbm = pl.BlockSpec(memory_space=pl.ANY)
    pairs = pltpu.SemaphoreType.DMA((peers - 1,))
    return pl.pallas_call(
        functools.partial(fused_kernel, nb, nu),
        out_shape=jax.ShapeDtypeStruct(queries.shape, jnp.bfloat16),
        in_specs=[hbm] * 9,
        out_specs=hbm,
        scratch_shapes=[
            pltpu.VMEM((3, rows, features), jnp.bfloat16),
            pltpu.VMEM((peers - 1, own, 3, rows, HD), jnp.bfloat16),
            pltpu.VMEM((peers, own, 3, rows, HD), jnp.bfloat16),
            pltpu.VMEM((2, tokens, width), jnp.bfloat16),
            pltpu.VMEM((step_gates.shape[0], width), jnp.bfloat16),
            pltpu.VMEM((tokens, width), jnp.bfloat16),
            pltpu.SMEM(positions.shape, jnp.int32),
            pltpu.SMEM(exponents.shape, jnp.int32),
            pltpu.SMEM(step_index.shape, jnp.int32),
            pltpu.SemaphoreType.DMA((10,)),
            pairs,
            pairs,
            pairs,
            pairs,
        ],
        compiler_params=pltpu.CompilerParams(collective_id=0, has_side_effects=True),
    )(*args)


def solution(mesh):
    nb, nu = mesh.shape["blk"], mesh.shape["ulysses"]

    def body(*args):
        heads = args[3].shape[2] // HD
        block = args[3].shape[1] // args[6].shape[2]
        if heads % nb == 0 and nb * nu > 1 and block % args[0].shape[1] == 0:
            return fused(nb, nu, *args)
        return shards(*args)

    return jax.shard_map(
        body,
        mesh=mesh,
        in_specs=(
            P("cfg", ("groups", "blk", "ulysses"), None),
            P("cfg", ("groups", "blk", "ulysses"), None),
            P("cfg", ("groups", "blk", "ulysses"), None),
            P("cfg", "groups", "ulysses"),
            P("cfg", "groups", "ulysses"),
            P(("groups", "blk", "ulysses")),
            P(None, "cfg", "groups", "ulysses"),
            P("groups"),
            P(None, "ulysses"),
        ),
        out_specs=P("cfg", ("groups", "blk", "ulysses"), None),
        check_vma=False,
    )
```

```python
import functools
import math

import jax
import jax.numpy as jnp
from jax import lax
from jax.experimental import pallas as pl
from jax.experimental.pallas import tpu as pltpu
from jax.sharding import PartitionSpec as P

HD = 128
BLOCK = 32
GRID_H = 16
GRID_W = 16
MESH = pl.DeviceIdType.MESH


def angles(positions):
    pair_count = HD // 2
    side_pairs = HD // 6
    frame_pairs = pair_count - 2 * side_pairs
    frame_index = (positions // (GRID_H * GRID_W)).astype(jnp.float32)
    row_index = (positions // GRID_W % GRID_H).astype(jnp.float32)
    column_index = (positions % GRID_W).astype(jnp.float32)

    def frequencies(count):
        return jnp.exp(-math.log(10000.0) * jnp.arange(count, dtype=jnp.float32) / count)

    phases = jnp.concatenate(
        [
            frame_index[:, None] * frequencies(frame_pairs)[None, :],
            row_index[:, None] * frequencies(side_pairs)[None, :],
            column_index[:, None] * frequencies(side_pairs)[None, :],
        ],
        axis=1,
    )
    return (jnp.cos(phases), jnp.sin(phases))


def rotate(source, cosine, sine):
    leading = source.shape[:-1]
    head_count = source.shape[-1] // HD
    paired = source.astype(jnp.float32).reshape(leading + (head_count, HD // 2, 2))
    real_part = paired[..., 0]
    imag_part = paired[..., 1]
    cos_part = cosine[:, None, :]
    sin_part = sine[:, None, :]
    turned = jnp.stack(
        [real_part * cos_part - imag_part * sin_part, real_part * sin_part + imag_part * cos_part],
        axis=-1,
    )
    return turned.reshape(source.shape)


def shards(
    queries,
    key_now,
    value_now,
    key_stale,
    value_stale,
    positions,
    exponents,
    step_index,
    step_gates,
):
    cosine, sine = angles(positions)
    query_turned = rotate(queries[0], cosine, sine).astype(jnp.bfloat16)
    key_turned = rotate(key_now[0], cosine, sine).astype(jnp.bfloat16)
    query_local, key_local, value_local = (
        lax.all_to_all(query_turned, "ulysses", split_axis=1, concat_axis=0, tiled=True),
        lax.all_to_all(key_turned, "ulysses", split_axis=1, concat_axis=0, tiled=True),
        lax.all_to_all(value_now[0], "ulysses", split_axis=1, concat_axis=0, tiled=True),
    )
    tok_rows = query_local.shape[0]
    feature_width = query_local.shape[1]
    head_count = feature_width // HD
    all_rows = key_stale.shape[1]
    first_row = lax.axis_index("blk") * tok_rows
    powers = jnp.repeat(jnp.exp2(exponents[:, 0].astype(jnp.float32)), BLOCK, axis=1)
    inverses = jnp.repeat(jnp.exp2(-exponents[:, 0].astype(jnp.float32)), BLOCK, axis=1)
    stale_keys = key_stale[0]
    stale_values = value_stale[0]

    def encode(current, stale, inverse):
        own_stale = lax.dynamic_slice_in_dim(stale, first_row, tok_rows, 0).astype(jnp.float32)
        own_inverse = lax.dynamic_slice_in_dim(inverse, first_row, tok_rows, 0)
        difference = (
            current.astype(jnp.float32).reshape(tok_rows, head_count, HD)
            - own_stale.reshape(tok_rows, head_count, HD)
        ) * own_inverse[:, :, None]
        return (
            jnp.clip(difference, -448.0, 448.0)
            .astype(jnp.bfloat16)
            .reshape(tok_rows, feature_width)
        )

    key_sent = encode(key_local, stale_keys, inverses[0])
    value_sent = encode(value_local, stale_values, inverses[1])
    query_heads = query_local.reshape(tok_rows, head_count, HD)
    score_scale = 1.0 / math.sqrt(HD)
    stale_scores = jnp.einsum(
        "qhd,khd->hqk",
        query_heads,
        stale_keys.reshape(all_rows, head_count, HD),
        preferred_element_type=jnp.float32,
    )
    key_whole, value_whole = (
        lax.all_gather(key_sent, "blk", axis=0, tiled=True),
        lax.all_gather(value_sent, "blk", axis=0, tiled=True),
    )
    span_rows = key_whole.shape[0]
    scaling = powers[0]
    residual = key_whole.reshape(span_rows, head_count, HD)
    scaled = (residual.astype(jnp.float32) * scaling[:, :, None]).astype(jnp.bfloat16)
    fresh_scores = jnp.einsum(
        "qhd,khd->hqk", query_heads, scaled, preferred_element_type=jnp.float32
    )
    scores = (stale_scores + fresh_scores) * score_scale
    peak_score = jnp.max(scores, axis=2, keepdims=True)
    weights = jnp.exp(scores - peak_score).astype(jnp.bfloat16)
    weight_total = jnp.sum(weights.astype(jnp.float32), axis=2)
    stale_sums = jnp.einsum(
        "hqk,khd->qhd",
        weights,
        stale_values.reshape(all_rows, head_count, HD),
        preferred_element_type=jnp.float32,
    )
    span_rows = value_whole.shape[0]
    scaling = powers[1]
    residual = value_whole.reshape(span_rows, head_count, HD)
    scaled = (residual.astype(jnp.float32) * scaling[:, :, None]).astype(jnp.bfloat16)
    fresh_sums = jnp.einsum("hqk,khd->qhd", weights, scaled, preferred_element_type=jnp.float32)
    mixture = (stale_sums + fresh_sums) / weight_total.T[:, :, None]
    gate_row = lax.dynamic_index_in_dim(step_gates, step_index[0], 0, keepdims=False).astype(
        jnp.float32
    )
    gated = (mixture * gate_row.reshape(head_count, HD)[None, :, :]).astype(jnp.bfloat16)
    restored = lax.all_to_all(
        gated.reshape(tok_rows, feature_width), "ulysses", split_axis=0, concat_axis=1, tiled=True
    )
    return restored[None]


def fused_kernel(
    nb,
    nu,
    q_ref,
    k_ref,
    v_ref,
    ks_ref,
    vs_ref,
    pos_hbm,
    exp_hbm,
    step_hbm,
    gates_ref,
    out_ref,
    qkv_in,
    send,
    recv,
    stale,
    gates,
    mixed,
    pos_ref,
    exp_ref,
    step_ref,
    in_sem,
    fwd_send,
    fwd_recv,
    ret_send,
    ret_recv,
):
    rows = q_ref.shape[1]
    tokens = ks_ref.shape[1]
    blocks = exp_ref.shape[2]
    block = tokens // blocks
    own = send.shape[1]
    width = own * HD
    b = lax.axis_index("blk")
    u = lax.axis_index("ulysses")
    rank = u * nb + b
    place_of = b * nu + u
    offsets = [(db, du) for db in range(nb) for du in range(nu) if (db, du) != (0, 0)]
    offsets.sort(key=lambda pair: (-min(pair[0], nb - pair[0]), -pair[1]))

    def ahead(db, du):
        return lax.rem(b + db, nb), lax.rem(u + du, nu)

    def behind(db, du):
        return lax.rem(b + nb - db, nb), lax.rem(u + nu - du, nu)

    def token_rows(bb, uu):
        return pl.ds(pl.multiple_of((bb * nu + uu) * rows, rows), rows)

    def head_columns(of_rank):
        return pl.ds(pl.multiple_of(of_rank * width, width), width)

    barrier = pltpu.get_barrier_semaphore()
    for db, du in offsets:
        bb, uu = ahead(db, du)
        pl.semaphore_signal(
            barrier, inc=1, device_id={"blk": bb, "ulysses": uu}, device_id_type=MESH
        )

    columns = head_columns(b)
    loads = [
        pltpu.make_async_copy(pos_hbm, pos_ref, in_sem.at[0]),
        pltpu.make_async_copy(q_ref.at[0], qkv_in.at[0], in_sem.at[1]),
        pltpu.make_async_copy(k_ref.at[0], qkv_in.at[1], in_sem.at[2]),
        pltpu.make_async_copy(v_ref.at[0], qkv_in.at[2], in_sem.at[3]),
        pltpu.make_async_copy(exp_hbm, exp_ref, in_sem.at[4]),
        pltpu.make_async_copy(step_hbm, step_ref, in_sem.at[5]),
        pltpu.make_async_copy(ks_ref.at[0, :, columns], stale.at[0], in_sem.at[6]),
        pltpu.make_async_copy(vs_ref.at[0, :, columns], stale.at[1], in_sem.at[7]),
        pltpu.make_async_copy(gates_ref.at[:, columns], gates, in_sem.at[8]),
    ]
    for load in loads[:4]:
        load.start()

    side = HD // 6
    front = HD // 2 - 2 * side
    lane = lax.broadcasted_iota(jnp.int32, (rows, HD), 1)
    row = lax.broadcasted_iota(jnp.int32, (rows, HD), 0)
    pair = lane >> 1
    even = (lane & 1) == 0
    in_front = pair < front
    in_rows = pair < front + side
    within = jnp.where(in_front, pair, jnp.where(in_rows, pair - front, pair - front - side))
    count = jnp.where(in_front, float(front), float(side))
    frequency = jnp.exp(-math.log(10000.0) * within.astype(jnp.float32) / count)
    loads[0].wait()
    position = jnp.zeros((rows, HD), jnp.int32)
    for t in range(rows):
        position = jnp.where(row == t, pos_ref[t], position)
    place = jnp.where(
        in_front,
        position // (GRID_H * GRID_W),
        jnp.where(in_rows, position // GRID_W % GRID_H, position % GRID_W),
    ).astype(jnp.float32)
    phase = place * frequency
    cosine = jnp.cos(phase)
    sine = jnp.sin(phase)
    sine = jnp.where(even, -sine, sine)

    for load in loads[1:4]:
        load.wait()

    def turned(which, head):
        x = qkv_in[which, :, pl.ds(pl.multiple_of(head * HD, HD), HD)].astype(jnp.float32)
        other = jnp.where(even, pltpu.roll(x, HD - 1, 1), pltpu.roll(x, 1, 1))
        return (x * cosine + other * sine).astype(jnp.bfloat16)

    def fill(target, to_rank):
        for j in range(own):
            head = to_rank * own + j
            target[j, 0] = turned(0, head)
            target[j, 1] = turned(1, head)
            target[j, 2] = qkv_in[2, :, pl.ds(pl.multiple_of(head * HD, HD), HD)]

    def forward(i, db, du):
        bb, uu = ahead(db, du)
        return pltpu.make_async_remote_copy(
            src_ref=send.at[i],
            dst_ref=recv.at[place_of],
            send_sem=fwd_send.at[i],
            recv_sem=fwd_recv.at[i],
            device_id={"blk": bb, "ulysses": uu},
            device_id_type=MESH,
        )

    for i, (db, du) in enumerate(offsets):
        bb, uu = ahead(db, du)
        fill(send.at[i], uu * nb + bb)
        if i == 0:
            pl.semaphore_wait(barrier, len(offsets))
        forward(i, db, du).start()
    for load in loads[4:]:
        load.start()
    fill(recv.at[place_of], rank)

    for load in loads[4:]:
        load.wait()
    chosen = lax.broadcasted_iota(jnp.int32, gates.shape, 0) == step_ref[0]
    gate_row = jnp.sum(
        jnp.where(chosen, gates[...].astype(jnp.float32), 0.0), axis=0, keepdims=True
    )

    def residual(which, j):
        at = slice(j * HD, (j + 1) * HD)
        parts = []
        per = block // rows
        for n in range(blocks):
            span = slice(n * block, (n + 1) * block)
            exponent = jnp.full((block, HD), exp_ref[which, 0, n, b * own + j], jnp.int32)
            one = jnp.ones_like(exponent)
            inverse = lax.shift_left(one, -exponent).astype(jnp.float32)
            power = lax.shift_left(one, exponent + 16).astype(jnp.float32) * 2.0**-16
            now = jnp.concatenate(
                [recv[n * per + m, j, 1 + which] for m in range(per)], axis=0
            ).astype(jnp.float32)
            before = stale[which, span, at].astype(jnp.float32)
            sent = jnp.clip((now - before) * inverse, -448.0, 448.0).astype(jnp.bfloat16)
            parts.append((sent.astype(jnp.float32) * power).astype(jnp.bfloat16))
        return jnp.concatenate(parts, axis=0)

    for i, (db, du) in enumerate(offsets):
        bb, uu = behind(db, du)
        pltpu.make_async_remote_copy(
            src_ref=send.at[i],
            dst_ref=recv.at[bb * nu + uu],
            send_sem=fwd_send.at[i],
            recv_sem=fwd_recv.at[i],
            device_id={"blk": bb, "ulysses": uu},
            device_id_type=MESH,
        ).wait_recv()

    for j in range(own):
        at = slice(j * HD, (j + 1) * HD)
        query = jnp.concatenate([recv[t, j, 0] for t in range(nb * nu)], axis=0)
        keys = jnp.concatenate([stale[0, :, at], residual(0, j)], axis=1)
        scores = lax.dot_general(
            jnp.concatenate([query, query], axis=1),
            keys,
            (((1,), (1,)), ((), ())),
            preferred_element_type=jnp.float32,
        ) * (1.0 / math.sqrt(HD))
        peak = jnp.max(scores, axis=1, keepdims=True)
        weights = jnp.exp(scores - peak).astype(jnp.bfloat16)
        total = jnp.sum(weights.astype(jnp.float32), axis=1, keepdims=True)
        values = jnp.concatenate([stale[1, :, at], residual(1, j)], axis=0)
        sums = jnp.dot(
            jnp.concatenate([weights, weights], axis=1),
            values,
            preferred_element_type=jnp.float32,
        )
        mixed[:, at] = (sums / total * gate_row[:, at]).astype(jnp.bfloat16)

    def back(i, db, du):
        bb, uu = ahead(db, du)
        return pltpu.make_async_remote_copy(
            src_ref=mixed.at[token_rows(bb, uu)],
            dst_ref=out_ref.at[0, :, head_columns(rank)],
            send_sem=ret_send.at[i],
            recv_sem=ret_recv.at[i],
            device_id={"blk": bb, "ulysses": uu},
            device_id_type=MESH,
        )

    for i, (db, du) in enumerate(offsets):
        back(i, db, du).start()
    kept = pltpu.make_async_copy(
        mixed.at[token_rows(b, u)], out_ref.at[0, :, head_columns(rank)], in_sem.at[9]
    )
    kept.start()
    for i, (db, du) in enumerate(offsets):
        bb, uu = behind(db, du)
        pltpu.make_async_remote_copy(
            src_ref=mixed.at[token_rows(b, u)],
            dst_ref=out_ref.at[0, :, head_columns(uu * nb + bb)],
            send_sem=ret_send.at[i],
            recv_sem=ret_recv.at[i],
            device_id={"blk": bb, "ulysses": uu},
            device_id_type=MESH,
        ).wait_recv()
    for i, (db, du) in enumerate(offsets):
        back(i, db, du).wait_send()
        forward(i, db, du).wait_send()
    kept.wait()


def fused(nb, nu, *args):
    queries, key_stale, positions, exponents, step_index, step_gates = (
        args[0],
        args[3],
        *args[5:],
    )
    rows, features = queries.shape[1:]
    tokens, columns = key_stale.shape[1:]
    own = columns // HD // nb
    width = own * HD
    peers = nb * nu
    hbm = pl.BlockSpec(memory_space=pl.ANY)
    pairs = pltpu.SemaphoreType.DMA((peers - 1,))
    return pl.pallas_call(
        functools.partial(fused_kernel, nb, nu),
        out_shape=jax.ShapeDtypeStruct(queries.shape, jnp.bfloat16),
        in_specs=[hbm] * 9,
        out_specs=hbm,
        scratch_shapes=[
            pltpu.VMEM((3, rows, features), jnp.bfloat16),
            pltpu.VMEM((peers - 1, own, 3, rows, HD), jnp.bfloat16),
            pltpu.VMEM((peers, own, 3, rows, HD), jnp.bfloat16),
            pltpu.VMEM((2, tokens, width), jnp.bfloat16),
            pltpu.VMEM((step_gates.shape[0], width), jnp.bfloat16),
            pltpu.VMEM((tokens, width), jnp.bfloat16),
            pltpu.SMEM(positions.shape, jnp.int32),
            pltpu.SMEM(exponents.shape, jnp.int32),
            pltpu.SMEM(step_index.shape, jnp.int32),
            pltpu.SemaphoreType.DMA((10,)),
            pairs,
            pairs,
            pairs,
            pairs,
        ],
        compiler_params=pltpu.CompilerParams(collective_id=0, has_side_effects=True),
    )(*args)


def solution(mesh):
    nb, nu = mesh.shape["blk"], mesh.shape["ulysses"]

    def body(*args):
        heads = args[3].shape[2] // HD
        block = args[3].shape[1] // args[6].shape[2]
        if heads % nb == 0 and nb * nu > 1 and block % args[0].shape[1] == 0:
            return fused(nb, nu, *args)
        return shards(*args)

    return jax.shard_map(
        body,
        mesh=mesh,
        in_specs=(
            P("cfg", ("groups", "blk", "ulysses"), None),
            P("cfg", ("groups", "blk", "ulysses"), None),
            P("cfg", ("groups", "blk", "ulysses"), None),
            P("cfg", "groups", "ulysses"),
            P("cfg", "groups", "ulysses"),
            P(("groups", "blk", "ulysses")),
            P(None, "cfg", "groups", "ulysses"),
            P("groups"),
            P(None, "ulysses"),
        ),
        out_specs=P("cfg", ("groups", "blk", "ulysses"), None),
        check_vma=False,
    )
```

```python
import functools
import math

import jax
import jax.numpy as jnp
from jax import lax
from jax.experimental import pallas as pl
from jax.experimental.pallas import tpu as pltpu
from jax.sharding import PartitionSpec as P

HD = 128
BLOCK = 32
GRID_H = 16
GRID_W = 16
MESH = pl.DeviceIdType.MESH


def angles(positions):
    pair_count = HD // 2
    side_pairs = HD // 6
    frame_pairs = pair_count - 2 * side_pairs
    frame_index = (positions // (GRID_H * GRID_W)).astype(jnp.float32)
    row_index = (positions // GRID_W % GRID_H).astype(jnp.float32)
    column_index = (positions % GRID_W).astype(jnp.float32)

    def frequencies(count):
        return jnp.exp(-math.log(10000.0) * jnp.arange(count, dtype=jnp.float32) / count)

    phases = jnp.concatenate(
        [
            frame_index[:, None] * frequencies(frame_pairs)[None, :],
            row_index[:, None] * frequencies(side_pairs)[None, :],
            column_index[:, None] * frequencies(side_pairs)[None, :],
        ],
        axis=1,
    )
    return (jnp.cos(phases), jnp.sin(phases))


def rotate(source, cosine, sine):
    leading = source.shape[:-1]
    head_count = source.shape[-1] // HD
    paired = source.astype(jnp.float32).reshape(leading + (head_count, HD // 2, 2))
    real_part = paired[..., 0]
    imag_part = paired[..., 1]
    cos_part = cosine[:, None, :]
    sin_part = sine[:, None, :]
    turned = jnp.stack(
        [real_part * cos_part - imag_part * sin_part, real_part * sin_part + imag_part * cos_part],
        axis=-1,
    )
    return turned.reshape(source.shape)


def shards(
    queries,
    key_now,
    value_now,
    key_stale,
    value_stale,
    positions,
    exponents,
    step_index,
    step_gates,
):
    cosine, sine = angles(positions)
    query_turned = rotate(queries[0], cosine, sine).astype(jnp.bfloat16)
    key_turned = rotate(key_now[0], cosine, sine).astype(jnp.bfloat16)
    query_local, key_local, value_local = (
        lax.all_to_all(query_turned, "ulysses", split_axis=1, concat_axis=0, tiled=True),
        lax.all_to_all(key_turned, "ulysses", split_axis=1, concat_axis=0, tiled=True),
        lax.all_to_all(value_now[0], "ulysses", split_axis=1, concat_axis=0, tiled=True),
    )
    tok_rows = query_local.shape[0]
    feature_width = query_local.shape[1]
    head_count = feature_width // HD
    all_rows = key_stale.shape[1]
    first_row = lax.axis_index("blk") * tok_rows
    powers = jnp.repeat(jnp.exp2(exponents[:, 0].astype(jnp.float32)), BLOCK, axis=1)
    inverses = jnp.repeat(jnp.exp2(-exponents[:, 0].astype(jnp.float32)), BLOCK, axis=1)
    stale_keys = key_stale[0]
    stale_values = value_stale[0]

    def encode(current, stale, inverse):
        own_stale = lax.dynamic_slice_in_dim(stale, first_row, tok_rows, 0).astype(jnp.float32)
        own_inverse = lax.dynamic_slice_in_dim(inverse, first_row, tok_rows, 0)
        difference = (
            current.astype(jnp.float32).reshape(tok_rows, head_count, HD)
            - own_stale.reshape(tok_rows, head_count, HD)
        ) * own_inverse[:, :, None]
        return (
            jnp.clip(difference, -448.0, 448.0)
            .astype(jnp.bfloat16)
            .reshape(tok_rows, feature_width)
        )

    key_sent = encode(key_local, stale_keys, inverses[0])
    value_sent = encode(value_local, stale_values, inverses[1])
    query_heads = query_local.reshape(tok_rows, head_count, HD)
    score_scale = 1.0 / math.sqrt(HD)
    stale_scores = jnp.einsum(
        "qhd,khd->hqk",
        query_heads,
        stale_keys.reshape(all_rows, head_count, HD),
        preferred_element_type=jnp.float32,
    )
    key_whole, value_whole = (
        lax.all_gather(key_sent, "blk", axis=0, tiled=True),
        lax.all_gather(value_sent, "blk", axis=0, tiled=True),
    )
    span_rows = key_whole.shape[0]
    scaling = powers[0]
    residual = key_whole.reshape(span_rows, head_count, HD)
    scaled = (residual.astype(jnp.float32) * scaling[:, :, None]).astype(jnp.bfloat16)
    fresh_scores = jnp.einsum(
        "qhd,khd->hqk", query_heads, scaled, preferred_element_type=jnp.float32
    )
    scores = (stale_scores + fresh_scores) * score_scale
    peak_score = jnp.max(scores, axis=2, keepdims=True)
    weights = jnp.exp(scores - peak_score).astype(jnp.bfloat16)
    weight_total = jnp.sum(weights.astype(jnp.float32), axis=2)
    stale_sums = jnp.einsum(
        "hqk,khd->qhd",
        weights,
        stale_values.reshape(all_rows, head_count, HD),
        preferred_element_type=jnp.float32,
    )
    span_rows = value_whole.shape[0]
    scaling = powers[1]
    residual = value_whole.reshape(span_rows, head_count, HD)
    scaled = (residual.astype(jnp.float32) * scaling[:, :, None]).astype(jnp.bfloat16)
    fresh_sums = jnp.einsum("hqk,khd->qhd", weights, scaled, preferred_element_type=jnp.float32)
    mixture = (stale_sums + fresh_sums) / weight_total.T[:, :, None]
    gate_row = lax.dynamic_index_in_dim(step_gates, step_index[0], 0, keepdims=False).astype(
        jnp.float32
    )
    gated = (mixture * gate_row.reshape(head_count, HD)[None, :, :]).astype(jnp.bfloat16)
    restored = lax.all_to_all(
        gated.reshape(tok_rows, feature_width), "ulysses", split_axis=0, concat_axis=1, tiled=True
    )
    return restored[None]


def fused_kernel(
    nb,
    nu,
    q_ref,
    k_ref,
    v_ref,
    ks_ref,
    vs_ref,
    pos_hbm,
    exp_hbm,
    step_hbm,
    gates_ref,
    out_ref,
    qkv_in,
    send,
    recv,
    stale,
    fresh,
    gates,
    mixed,
    pos_ref,
    exp_ref,
    step_ref,
    in_sem,
    fwd_send,
    fwd_recv,
    ret_send,
    ret_recv,
):
    rows = q_ref.shape[1]
    tokens = ks_ref.shape[1]
    blocks = exp_ref.shape[2]
    block = tokens // blocks
    own = send.shape[1]
    width = own * HD
    b = lax.axis_index("blk")
    u = lax.axis_index("ulysses")
    rank = u * nb + b
    place_of = b * nu + u
    offsets = [(db, du) for db in range(nb) for du in range(nu) if (db, du) != (0, 0)]
    offsets.sort(key=lambda pair: (-min(pair[0], nb - pair[0]), -pair[1]))

    def ahead(db, du):
        return lax.rem(b + db, nb), lax.rem(u + du, nu)

    def behind(db, du):
        return lax.rem(b + nb - db, nb), lax.rem(u + nu - du, nu)

    def token_rows(bb, uu):
        return pl.ds(pl.multiple_of((bb * nu + uu) * rows, rows), rows)

    def head_columns(of_rank):
        return pl.ds(pl.multiple_of(of_rank * width, width), width)

    barrier = pltpu.get_barrier_semaphore()
    for db, du in offsets:
        bb, uu = ahead(db, du)
        pl.semaphore_signal(
            barrier, inc=1, device_id={"blk": bb, "ulysses": uu}, device_id_type=MESH
        )

    columns = head_columns(b)
    loads = [
        pltpu.make_async_copy(pos_hbm, pos_ref, in_sem.at[0]),
        pltpu.make_async_copy(q_ref.at[0], qkv_in.at[0], in_sem.at[1]),
        pltpu.make_async_copy(k_ref.at[0], qkv_in.at[1], in_sem.at[2]),
        pltpu.make_async_copy(v_ref.at[0], qkv_in.at[2], in_sem.at[3]),
        pltpu.make_async_copy(exp_hbm, exp_ref, in_sem.at[4]),
        pltpu.make_async_copy(step_hbm, step_ref, in_sem.at[5]),
        pltpu.make_async_copy(ks_ref.at[0, :, columns], stale.at[0], in_sem.at[6]),
        pltpu.make_async_copy(vs_ref.at[0, :, columns], stale.at[1], in_sem.at[7]),
        pltpu.make_async_copy(gates_ref.at[:, columns], gates, in_sem.at[8]),
    ]
    for load in loads[:4]:
        load.start()

    side = HD // 6
    front = HD // 2 - 2 * side
    lane = lax.broadcasted_iota(jnp.int32, (rows, HD), 1)
    row = lax.broadcasted_iota(jnp.int32, (rows, HD), 0)
    pair = lane >> 1
    even = (lane & 1) == 0
    in_front = pair < front
    in_rows = pair < front + side
    within = jnp.where(in_front, pair, jnp.where(in_rows, pair - front, pair - front - side))
    count = jnp.where(in_front, float(front), float(side))
    frequency = jnp.exp(-math.log(10000.0) * within.astype(jnp.float32) / count)
    loads[0].wait()
    position = jnp.zeros((rows, HD), jnp.int32)
    for t in range(rows):
        position = jnp.where(row == t, pos_ref[t], position)
    place = jnp.where(
        in_front,
        position // (GRID_H * GRID_W),
        jnp.where(in_rows, position // GRID_W % GRID_H, position % GRID_W),
    ).astype(jnp.float32)
    phase = place * frequency
    cosine = jnp.cos(phase)
    sine = jnp.sin(phase)
    sine = jnp.where(even, -sine, sine)

    for load in loads[1:4]:
        load.wait()

    def turned(which, head):
        x = qkv_in[which, :, pl.ds(pl.multiple_of(head * HD, HD), HD)].astype(jnp.float32)
        other = jnp.where(even, pltpu.roll(x, HD - 1, 1), pltpu.roll(x, 1, 1))
        return (x * cosine + other * sine).astype(jnp.bfloat16)

    def fill(target, to_rank):
        for j in range(own):
            head = to_rank * own + j
            target[j, 0] = turned(0, head)
            target[j, 1] = turned(1, head)
            target[j, 2] = qkv_in[2, :, pl.ds(pl.multiple_of(head * HD, HD), HD)]

    def forward(i, db, du):
        bb, uu = ahead(db, du)
        return pltpu.make_async_remote_copy(
            src_ref=send.at[i],
            dst_ref=recv.at[place_of],
            send_sem=fwd_send.at[i],
            recv_sem=fwd_recv.at[i],
            device_id={"blk": bb, "ulysses": uu},
            device_id_type=MESH,
        )

    for i, (db, du) in enumerate(offsets):
        bb, uu = ahead(db, du)
        fill(send.at[i], uu * nb + bb)
        if i == 0:
            pl.semaphore_wait(barrier, len(offsets))
        forward(i, db, du).start()
    for load in loads[4:]:
        load.start()
    fill(recv.at[place_of], rank)

    for load in loads[4:]:
        load.wait()
    chosen = lax.broadcasted_iota(jnp.int32, gates.shape, 0) == step_ref[0]
    gate_row = jnp.sum(
        jnp.where(chosen, gates[...].astype(jnp.float32), 0.0), axis=0, keepdims=True
    )

    def encode(bb):
        span = pl.ds(pl.multiple_of(bb * nu * rows, nu * rows), nu * rows)
        block_of = bb * nu * rows // block
        for which in range(2):
            for j in range(own):
                at = slice(j * HD, (j + 1) * HD)
                exponent = jnp.full(
                    (nu * rows, HD), exp_ref[which, 0, block_of, b * own + j], jnp.int32
                )
                one = jnp.ones_like(exponent)
                inverse = lax.shift_left(one, -exponent).astype(jnp.float32)
                power = lax.shift_left(one, exponent + 16).astype(jnp.float32) * 2.0**-16
                now = jnp.concatenate(
                    [recv[bb * nu + m, j, 1 + which] for m in range(nu)], axis=0
                ).astype(jnp.float32)
                before = stale[which, span, at].astype(jnp.float32)
                sent = jnp.clip((now - before) * inverse, -448.0, 448.0).astype(jnp.bfloat16)
                fresh[which, span, at] = (sent.astype(jnp.float32) * power).astype(jnp.bfloat16)

    def arrived(i, db, du):
        bb, uu = behind(db, du)
        pltpu.make_async_remote_copy(
            src_ref=send.at[i],
            dst_ref=recv.at[bb * nu + uu],
            send_sem=fwd_send.at[i],
            recv_sem=fwd_recv.at[i],
            device_id={"blk": bb, "ulysses": uu},
            device_id_type=MESH,
        ).wait_recv()

    for distance in sorted(range(nb), key=lambda d: -min(d, nb - d) if d else -nb):
        for i, (db, du) in enumerate(offsets):
            if db == distance:
                arrived(i, db, du)
        encode(lax.rem(b + nb - distance, nb))

    for j in range(own):
        at = slice(j * HD, (j + 1) * HD)
        query = jnp.concatenate([recv[t, j, 0] for t in range(nb * nu)], axis=0)
        keys = jnp.concatenate([stale[0, :, at], fresh[0, :, at]], axis=1)
        scores = lax.dot_general(
            jnp.concatenate([query, query], axis=1),
            keys,
            (((1,), (1,)), ((), ())),
            preferred_element_type=jnp.float32,
        ) * (1.0 / math.sqrt(HD))
        peak = jnp.max(scores, axis=1, keepdims=True)
        weights = jnp.exp(scores - peak).astype(jnp.bfloat16)
        total = jnp.sum(weights.astype(jnp.float32), axis=1, keepdims=True)
        values = jnp.concatenate([stale[1, :, at], fresh[1, :, at]], axis=0)
        sums = jnp.dot(
            jnp.concatenate([weights, weights], axis=1),
            values,
            preferred_element_type=jnp.float32,
        )
        mixed[:, at] = (sums / total * gate_row[:, at]).astype(jnp.bfloat16)

    def back(i, db, du):
        bb, uu = ahead(db, du)
        return pltpu.make_async_remote_copy(
            src_ref=mixed.at[token_rows(bb, uu)],
            dst_ref=out_ref.at[0, :, head_columns(rank)],
            send_sem=ret_send.at[i],
            recv_sem=ret_recv.at[i],
            device_id={"blk": bb, "ulysses": uu},
            device_id_type=MESH,
        )

    for i, (db, du) in enumerate(offsets):
        back(i, db, du).start()
    kept = pltpu.make_async_copy(
        mixed.at[token_rows(b, u)], out_ref.at[0, :, head_columns(rank)], in_sem.at[9]
    )
    kept.start()
    for i, (db, du) in enumerate(offsets):
        forward(i, db, du).wait_send()
    for i, (db, du) in enumerate(offsets):
        bb, uu = behind(db, du)
        pltpu.make_async_remote_copy(
            src_ref=mixed.at[token_rows(b, u)],
            dst_ref=out_ref.at[0, :, head_columns(uu * nb + bb)],
            send_sem=ret_send.at[i],
            recv_sem=ret_recv.at[i],
            device_id={"blk": bb, "ulysses": uu},
            device_id_type=MESH,
        ).wait_recv()
    for i, (db, du) in enumerate(offsets):
        back(i, db, du).wait_send()
    kept.wait()


def fused(nb, nu, *args):
    queries, key_stale, positions, exponents, step_index, step_gates = (
        args[0],
        args[3],
        *args[5:],
    )
    rows, features = queries.shape[1:]
    tokens, columns = key_stale.shape[1:]
    own = columns // HD // nb
    width = own * HD
    peers = nb * nu
    hbm = pl.BlockSpec(memory_space=pl.ANY)
    pairs = pltpu.SemaphoreType.DMA((peers - 1,))
    return pl.pallas_call(
        functools.partial(fused_kernel, nb, nu),
        out_shape=jax.ShapeDtypeStruct(queries.shape, jnp.bfloat16),
        in_specs=[hbm] * 9,
        out_specs=hbm,
        scratch_shapes=[
            pltpu.VMEM((3, rows, features), jnp.bfloat16),
            pltpu.VMEM((peers - 1, own, 3, rows, HD), jnp.bfloat16),
            pltpu.VMEM((peers, own, 3, rows, HD), jnp.bfloat16),
            pltpu.VMEM((2, tokens, width), jnp.bfloat16),
            pltpu.VMEM((2, tokens, width), jnp.bfloat16),
            pltpu.VMEM((step_gates.shape[0], width), jnp.bfloat16),
            pltpu.VMEM((tokens, width), jnp.bfloat16),
            pltpu.SMEM(positions.shape, jnp.int32),
            pltpu.SMEM(exponents.shape, jnp.int32),
            pltpu.SMEM(step_index.shape, jnp.int32),
            pltpu.SemaphoreType.DMA((10,)),
            pairs,
            pairs,
            pairs,
            pairs,
        ],
        compiler_params=pltpu.CompilerParams(collective_id=0, has_side_effects=True),
    )(*args)


def solution(mesh):
    nb, nu = mesh.shape["blk"], mesh.shape["ulysses"]

    def body(*args):
        heads = args[3].shape[2] // HD
        block = args[3].shape[1] // args[6].shape[2]
        if heads % nb == 0 and nb * nu > 1 and block % (args[0].shape[1] * nu) == 0:
            return fused(nb, nu, *args)
        return shards(*args)

    return jax.shard_map(
        body,
        mesh=mesh,
        in_specs=(
            P("cfg", ("groups", "blk", "ulysses"), None),
            P("cfg", ("groups", "blk", "ulysses"), None),
            P("cfg", ("groups", "blk", "ulysses"), None),
            P("cfg", "groups", "ulysses"),
            P("cfg", "groups", "ulysses"),
            P(("groups", "blk", "ulysses")),
            P(None, "cfg", "groups", "ulysses"),
            P("groups"),
            P(None, "ulysses"),
        ),
        out_specs=P("cfg", ("groups", "blk", "ulysses"), None),
        check_vma=False,
    )
```
